32 devices in a mesh: groups: 2 (over y), heads: 4 (over x, core), tm: 4 (over z).
Axes of the slice: x: 2, y: 2, z: 4, core: 2. Of those that a mesh axis runs over, the one named last changes fastest.
Arguments:
- queries: bfloat16 [256, 8192], P('groups', 'heads'), parts along dimension 0, may hold values from -6 to 6
- cache_keys: bfloat16 [8192, 8192], P(('groups', 'tm'), 'heads'), parts along dimension 0, may hold values from -650 to 650
- cache_values: bfloat16 [8192, 8192], P(('groups', 'tm'), 'heads'), parts along dimension 0, may hold values from -6 to 6
- residual: bfloat16 [256, 8192], P('groups', 'tm'), parts along dimension 0, may hold values from -20 to 20
- out_weight: bfloat16 [8192, 8192], P('heads', 'tm'), may hold values from -0.0625 to 0.0625
- norm_gain: float32 [8192], P('tm'), may hold values from 0.1 to 1.9
- cond_weight: bfloat16 [8192, 1536], P('tm', 'heads'), may hold values from -0.0625 to 0.0625
- in_weight: bfloat16 [1152, 1536], replicated, may hold values from -0.1875 to 0.1875
- head_out: bfloat16 [1536, 1152], replicated, may hold values from -0.15625 to 0.15625
- start_state: float32 [256, 1152], P(('groups', 'heads')), parts along dimension 0, may hold values from -6 to 6
- noise_draws: bfloat16 [256, 8, 1152], P(('groups', 'heads'), 'tm'), parts along dimension 0, may hold values from -6 to 6
- positions: int32 [256], P('groups'), parts along dimension 0, may hold values from 0 to 4095
- cache_length: int32 [2], P('groups'), parts along dimension 0, may hold values from 2048 to 4096
- plan: int32 [9], replicated, may hold values from 0 to 1000, as said below
Outputs:
- states: float32 [256, 8, 1152], P(('groups', 'heads'), 'tm'), parts along dimension 0
The draws below stay inside these ranges and needn't reach their ends.
There are 2 independent parts, one for each index of `groups`. The reference program is written for one: setup_inputs(seed, part) draws one part's arguments, and reference() takes and returns one part's arrays. A program takes and returns all parts, laid end to end along the dimension named above; an argument that names none is the same for every part. Nothing has to cross between parts.
Inputs may be any that keep to these rules, and one draw needn't show every extreme that they name: `plan`: strictly decreasing; the first entry is 1000 and the last is 0.
All inputs are finite; a program needn't handle non-finite values.
Results may differ from the reference program's by a relative error of at most 0.0028.
Values may be sent and summed in bfloat16 or wider, within the bound.
A program may use at most 128 MiB of HBM per device.

```python
import math
import jax
import jax.numpy as jnp
from jax import lax

D = 8192
HEADS = 64
HD = 128
WIDTH = 1536
CHAN = 1152
CACHE_DEV = 1024
SWEEPS = 3
ROWS = 128
CACHE = 4096
TIMES = 8
N_TM = 4


def draw_plan(key, part):
    inner = jax.random.permutation(key, 999)[:TIMES - 1] + 1
    inner = -jnp.sort(-inner)
    return jnp.concatenate([jnp.array([1000], dtype=jnp.int32), inner.astype(jnp.int32), jnp.array([0], dtype=jnp.int32)])


def draw_cache_keys(key, part):
    key_one = jax.random.fold_in(jax.random.fold_in(key, 11), 0)
    base = jnp.clip(jax.random.normal(key_one, (CACHE, D), jnp.float32), -4.0, 4.0)
    return base.astype(jnp.bfloat16)


def draw_residual(key, part):
    key_one, key_two, key_three = jax.random.split(jax.random.fold_in(key, 23), 3)
    normal_part = jnp.clip(jax.random.normal(key_one, (ROWS, D), jnp.float32), -4.0, 4.0)
    row_scale = jnp.power(10.0, jax.random.uniform(key_two, (ROWS, 1), jnp.float32, -0.5, 0.5))
    column = jnp.arange(D, dtype=jnp.float32) / D
    col_scale = jnp.power(10.0, 0.4 * column - 0.2 + 0.2 * jax.random.uniform(key_three, (D,), jnp.float32, -1.0, 1.0))
    return (normal_part * row_scale * col_scale[None, :] / 3.0).astype(jnp.bfloat16)


def touch_ends(values, own_key, low, high):
    longest = values.shape.index(max(values.shape))
    spots = []
    for shift in (0, 1):
        where = [jax.random.randint(jax.random.fold_in(own_key, axis), (), 0, length) for axis, length in enumerate(values.shape)]
        where[longest] = (where[longest] + shift) % values.shape[longest]
        spots.append(tuple(where))
    return values.at[spots[0]].set(low).at[spots[1]].set(high)


def shard_levels(key, extent, shards, low, high):
    loudness = 1.0
    for position, shards_of in shards:
        steps = jax.random.uniform(jax.random.fold_in(jax.random.fold_in(key, 6), position), (shards_of,), jnp.float32, low / len(shards), high / len(shards))
        loudness = loudness * jnp.repeat(jnp.exp(steps), extent[position] // shards_of).reshape((-1,) + (1,) * (len(extent) - 1 - position))
    return loudness


def noise(rng, dims, deviation, most, cuts=(), kind=jnp.bfloat16):
    values = jax.random.normal(rng, dims, jnp.float32) * deviation
    if len(cuts) > 0:
        values = shard_levels(rng, dims, cuts, -0.22, 0.18) * values
    return jnp.clip(values, min=-most, max=most).astype(kind)


def setup_inputs(seed: int = 0, part: int = 0) -> dict:
    key_of = jax.random.split(jax.random.key(seed), 15)
    part_splits = jax.random.split(jax.random.fold_in(key_of[14], part), 15)
    return {
        "queries": noise(part_splits[0], (ROWS, D), 1.0, 6.0, ((1, 4),)),
        "cache_keys": draw_cache_keys(jax.random.fold_in(jax.random.fold_in(key_of[14], part), 71), part),
        "cache_values": noise(part_splits[2], (CACHE, D), 1.0, 6.0, ((0, 4), (1, 4))),
        "residual": draw_residual(jax.random.fold_in(jax.random.fold_in(key_of[14], part), 71), part),
        "out_weight": noise(key_of[4], (D, D), D ** -0.5, 0.0625, ((0, 4), (1, 4))),
        "norm_gain": jnp.clip(1.0 + 0.18 * jax.random.normal(key_of[5], (D,), jnp.float32), 0.1, 1.9),
        "cond_weight": noise(key_of[6], (D, WIDTH), D ** -0.5, 0.0625, ((0, 4), (1, 4))),
        "in_weight": noise(key_of[7], (CHAN, WIDTH), CHAN ** -0.5, 0.1875),
        "head_out": noise(key_of[8], (WIDTH, CHAN), WIDTH ** -0.5, 0.15625),
        "start_state": noise(part_splits[9], (ROWS, CHAN), 1.0, 6.0, ((0, 4),), jnp.float32),
        "noise_draws": noise(part_splits[10], (ROWS, TIMES, CHAN), 1.0, 6.0, ((0, 4), (1, 4))),
        "positions": touch_ends(jax.random.randint(part_splits[11], (ROWS,), 0, CACHE), jax.random.fold_in(part_splits[11], 1), 0, CACHE - 1).astype(jnp.int32),
        "cache_length": jax.random.randint(part_splits[12], (1,), CACHE // 2, CACHE + 1).astype(jnp.int32),
        "plan": draw_plan(jax.random.fold_in(key_of[14], 71), part),
    }


def rotate(values, angle_pos):
    head_feature_width = values.shape[-1]
    half_dim = head_feature_width // 2
    frequencies = jnp.exp(-math.log(10000.0) * 2.0 * jnp.arange(half_dim, dtype=jnp.float32) / head_feature_width)
    angles = angle_pos[:, None] * frequencies[None, :]
    cosine = jnp.cos(angles)[:, None, :]
    sine_part = jnp.sin(angles)[:, None, :]
    paired = values.astype(jnp.float32).reshape(values.shape[0], values.shape[1], half_dim, 2)
    real_part = paired[..., 0]
    imag_part = paired[..., 1]
    turned = jnp.stack([real_part * cosine - imag_part * sine_part, real_part * sine_part + imag_part * cosine], axis=-1)
    return turned.reshape(values.shape).astype(jnp.bfloat16)

def time_terms(levels, hidden_width):
    half_width = hidden_width // 2
    frequencies = jnp.exp(-math.log(10000.0) * jnp.arange(half_width, dtype=jnp.float32) / half_width)
    angles = levels[:-1, None] * frequencies[None, :]
    embedding = jnp.concatenate([jnp.sin(angles), jnp.cos(angles)], axis=1)
    step_size = (levels[:-1] - levels[1:]) / 1000.0
    return (embedding, step_size, jnp.sqrt(step_size))

def block_attend(rotary_applied, block_key_rows, block_value_rows, valid_keys):
    head_feature_width = rotary_applied.shape[-1]
    attention_logits = jnp.einsum('orp,brp->orb', rotary_applied.astype(jnp.float32), block_key_rows.astype(jnp.float32), precision=lax.Precision.HIGHEST) * (1.0 / math.sqrt(head_feature_width))
    masked = jnp.where(valid_keys[None, None, :], attention_logits, jnp.float32(-1e+30))
    block_max = lax.optimization_barrier(jnp.max(masked, axis=2))
    weights = jnp.where(valid_keys[None, None, :], jnp.exp(masked - block_max[:, :, None]), jnp.float32(0.0))
    block_total = lax.optimization_barrier(jnp.sum(weights, axis=2))
    rounded_values = weights.astype(jnp.bfloat16).astype(jnp.float32)
    block_output_part = jnp.einsum('pzu,uzx->pzx', rounded_values, block_value_rows.astype(jnp.float32), precision=lax.Precision.HIGHEST)
    return (block_max, block_total, block_output_part)

def reference(queries, cache_keys, cache_values, residual, out_weight, norm_gain, cond_weight, in_weight, head_out, start_state, noise_draws, positions, cache_length, plan):
    row_total = queries.shape[0]
    rotary_applied = rotate(queries.reshape(row_total, HEADS, HD), positions.astype(jnp.float32))

    def one_block(block_index):
        first_key = (block_index * CACHE_DEV).astype(jnp.int32)
        block_key_rows = lax.dynamic_slice_in_dim(cache_keys, first_key, CACHE_DEV, 0).reshape(CACHE_DEV, HEADS, HD)
        block_value_rows = lax.dynamic_slice_in_dim(cache_values, first_key, CACHE_DEV, 0).reshape(CACHE_DEV, HEADS, HD)
        key_pos = first_key + jnp.arange(CACHE_DEV, dtype=jnp.int32)
        valid_keys = key_pos < cache_length[0]
        return block_attend(rotary_applied, block_key_rows, block_value_rows, valid_keys)
    block_maxes, block_totals, block_outs = lax.map(one_block, jnp.arange(N_TM, dtype=jnp.int32))
    highest = lax.optimization_barrier(jnp.max(block_maxes, axis=0))
    factors = jnp.exp(block_maxes - highest[None])
    numer = lax.optimization_barrier(jnp.sum(block_outs * factors[..., None], axis=0))
    denom = lax.optimization_barrier(jnp.sum(block_totals * factors, axis=0))
    attended = (numer / denom[:, :, None]).reshape(row_total, D).astype(jnp.bfloat16)
    hidden = residual.astype(jnp.float32) + jnp.dot(attended, out_weight, preferred_element_type=jnp.float32)
    inverse = lax.rsqrt(lax.optimization_barrier(jnp.mean(hidden * hidden, axis=1)) + 1e-06)
    scaled = (hidden * norm_gain[None, :]).astype(jnp.bfloat16)
    condition = inverse[:, None] * jnp.dot(scaled, cond_weight, preferred_element_type=jnp.float32)
    embedding, step_size, noise_scale = time_terms(plan.astype(jnp.float32), WIDTH)
    time_total = noise_draws.shape[1]
    noise_term = noise_scale[None, :, None] * noise_draws.astype(jnp.float32)
    states = jnp.broadcast_to(start_state[:, None, :], noise_draws.shape).astype(jnp.float32)
    for sweep_index in range(SWEEPS):
        flat_states = states.astype(jnp.bfloat16).reshape(row_total * time_total, CHAN)
        preact = jnp.dot(flat_states, in_weight, preferred_element_type=jnp.float32).reshape(row_total, time_total, WIDTH)
        preact = preact + condition[:, None, :] + embedding[None]
        action = jax.nn.silu(preact).astype(jnp.bfloat16)
        drift_term = jnp.dot(action.reshape(row_total * time_total, WIDTH), head_out, preferred_element_type=jnp.float32).reshape(row_total, time_total, CHAN)
        increment = step_size[None, :, None] * drift_term + noise_term
        running = jnp.cumsum(increment, axis=1)
        states = start_state[:, None, :] + (running - increment)
    return states
```

```python
import functools
import math

import jax
import jax.numpy as jnp
from jax import lax
from jax.experimental import pallas as pl
from jax.experimental.pallas import tpu as pltpu
from jax.sharding import PartitionSpec as P

HD = 128
SWEEPS = 3
LANES = 128
F32 = jnp.float32
BF16 = jnp.bfloat16
VMEM = pl.BlockSpec(memory_space=pltpu.VMEM)
LIMIT = 56 * 1024 * 1024


def greet(axes):
    barrier = pltpu.get_barrier_semaphore()
    count = 0
    for axis in axes:
        n = lax.axis_size(axis)
        me = lax.axis_index(axis)
        for step in range(1, n):
            pl.semaphore_signal(
                barrier,
                inc=1,
                device_id={axis: lax.rem(me + step, n)},
                device_id_type=pl.DeviceIdType.MESH,
            )
        count += n - 1
    pl.semaphore_wait(barrier, count)


def spread(axis, source, target, send, recv):
    n = lax.axis_size(axis)
    me = lax.axis_index(axis)
    copies = []
    for step in range(1, n):
        partner = lax.rem(me + step, n)
        copy = pltpu.make_async_remote_copy(
            src_ref=source(partner),
            dst_ref=target(me),
            send_sem=send.at[step],
            recv_sem=recv.at[step],
            device_id={axis: partner},
            device_id_type=pl.DeviceIdType.MESH,
        )
        copy.start()
        copies.append(copy)
    return copies


def rows_of(index, size):
    return pl.ds(pl.multiple_of(index * size, size), size)


def attend_kernel(valid_ref, q_ref, cos_ref, sin_ref, k_ref, v_ref, out_ref, stats_ref):
    head = pl.program_id(0)
    q = q_ref[...].astype(F32)
    lane = lax.broadcasted_iota(jnp.int32, q.shape, 1)
    other = jnp.where(lane % 2 == 0, -pltpu.roll(q, HD - 1, 1), pltpu.roll(q, 1, 1))
    rotated = (q * cos_ref[...] + other * sin_ref[...]).astype(BF16)
    scores = lax.dot_general(
        rotated, k_ref[...], (((1,), (1,)), ((), ())), preferred_element_type=F32
    ) * (1.0 / math.sqrt(HD))
    valid = lax.broadcasted_iota(jnp.int32, scores.shape, 1) < valid_ref[0]
    masked = jnp.where(valid, scores, F32(-1e30))
    top = jnp.max(masked, axis=1, keepdims=True)
    weights = jnp.where(valid, jnp.exp(masked - top), F32(0.0))
    total = jnp.sum(weights, axis=1, keepdims=True)
    out_ref[...] = jnp.dot(
        weights.astype(BF16), v_ref[...], preferred_element_type=F32
    ).astype(BF16)

    @pl.when(head == 0)
    def _():
        stats_ref[...] = jnp.zeros_like(stats_ref)

    lanes = lax.broadcasted_iota(jnp.int32, stats_ref.shape, 1)
    stats_ref[...] = jnp.where(
        lanes == head, top, jnp.where(lanes == head + LANES // 2, total, stats_ref[...])
    )


def attend(queries, cosine, sine, keys, values, valid):
    rows, width = queries.shape
    count = keys.shape[0]
    per_head = lambda size: pl.BlockSpec((size, HD), lambda h, _: (0, h))
    fixed = lambda: pl.BlockSpec((rows, LANES), lambda h, _: (0, 0))
    return pl.pallas_call(
        attend_kernel,
        grid_spec=pltpu.PrefetchScalarGridSpec(
            num_scalar_prefetch=1,
            grid=(width // HD,),
            in_specs=[per_head(rows), fixed(), fixed(), per_head(count), per_head(count)],
            out_specs=[per_head(rows), fixed()],
        ),
        out_shape=[
            jax.ShapeDtypeStruct((rows, width), BF16),
            jax.ShapeDtypeStruct((rows, LANES), F32),
        ],
        compiler_params=pltpu.CompilerParams(vmem_limit_bytes=LIMIT),
        cost_estimate=pl.CostEstimate(
            flops=4 * rows * count * width,
            bytes_accessed=4 * count * width,
            transcendentals=rows * count * (width // HD),
        ),
    )(valid, queries, cosine, sine, keys, values)


def merge_kernel(out_ref, stats_ref, att_ref, parts, stats, s1, r1, s2, r2, s3, r3):
    n = lax.axis_size("tm")
    me = lax.axis_index("tm")
    rows, width = out_ref.shape
    each = rows // n
    greet(["tm"])
    copies = spread(
        "tm", lambda p: stats_ref.at[rows_of(p, each)], lambda m: stats.at[m], s1, r1
    )
    copies += spread(
        "tm", lambda p: out_ref.at[rows_of(p, each)], lambda m: parts.at[m], s2, r2
    )
    stats[me] = stats_ref[rows_of(me, each), :]
    parts[me] = out_ref[rows_of(me, each), :]
    for copy in copies:
        copy.wait()
    half = LANES // 2
    tops = [stats[i][:, :half] for i in range(n)]
    top = functools.reduce(jnp.maximum, tops)
    factors = [jnp.exp(t - top) for t in tops]
    denom = sum(stats[i][:, half:] * factors[i] for i in range(n))
    mine = rows_of(me, each)
    for head in range(width // HD):
        cols = slice(head * HD, (head + 1) * HD)
        lane = slice(head, head + 1)
        numer = sum(parts[i, :, cols].astype(F32) * factors[i][:, lane] for i in range(n))
        att_ref[mine, cols] = (numer / denom[:, lane]).astype(BF16)
    for copy in spread(
        "tm", lambda p: att_ref.at[mine], lambda m: att_ref.at[rows_of(m, each)], s3, r3
    ):
        copy.wait()


def sems(*axes):
    return [pltpu.SemaphoreType.DMA((lax.axis_size(a),)) for a in axes for _ in range(2)]


def comm_params(ident):
    return pltpu.CompilerParams(
        collective_id=ident, has_side_effects=True, vmem_limit_bytes=LIMIT
    )


def merge(out, stats):
    n = lax.axis_size("tm")
    rows, width = out.shape
    return pl.pallas_call(
        merge_kernel,
        out_shape=jax.ShapeDtypeStruct((rows, width), BF16),
        in_specs=[VMEM] * 2,
        out_specs=VMEM,
        scratch_shapes=[
            pltpu.VMEM((n, rows // n, width), BF16),
            pltpu.VMEM((n, rows // n, LANES), F32),
        ]
        + sems("tm", "tm", "tm"),
        compiler_params=comm_params(1),
    )(out, stats)


def hidden_kernel(
    part_ref, res_ref, gain_ref, noise_ref, scaled_ref, square_ref, got_ref, parts, s1, r1, s2, r2
):
    n = lax.axis_size("heads")
    me = lax.axis_index("heads")
    when = lax.axis_index("tm")
    each = res_ref.shape[0]
    greet(["heads", "tm"])
    copies = spread(
        "heads", lambda p: part_ref.at[rows_of(p, each)], lambda m: parts.at[m], s1, r1
    )
    others = spread("tm", lambda p: noise_ref.at[p], lambda m: got_ref.at[m], s2, r2)
    parts[me] = part_ref[rows_of(me, each), :]
    got_ref[when] = noise_ref[when]
    for copy in copies:
        copy.wait()
    hidden = res_ref[...].astype(F32) + sum(parts[i].astype(F32) for i in range(n))
    squares = jnp.sum(hidden * hidden, axis=1, keepdims=True)
    square_ref[...] = jnp.broadcast_to(squares, square_ref.shape)
    scaled_ref[...] = (hidden * gain_ref[...]).astype(BF16)
    for copy in others:
        copy.wait()


def hidden_rows(partial, residual, gain, noise):
    n = lax.axis_size("heads")
    each, width = residual.shape
    return pl.pallas_call(
        hidden_kernel,
        out_shape=[
            jax.ShapeDtypeStruct((each, width), BF16),
            jax.ShapeDtypeStruct((each, LANES), F32),
            jax.ShapeDtypeStruct(noise.shape, noise.dtype),
        ],
        in_specs=[VMEM] * 4,
        out_specs=[VMEM] * 3,
        scratch_shapes=[pltpu.VMEM((n, each, width), BF16)] + sems("heads", "tm"),
        compiler_params=comm_params(2),
    )(partial, residual, gain, noise)


def sweep_kernel(
    model_width, cond_ref, square_ref, start_ref, emb_ref, step_ref, noise_ref, in_ref, head_ref,
    out_ref, conds, squares, base, states, low, action, s1, r1, s2, r2, s3, r3,
):
    n = lax.axis_size("tm")
    me = lax.axis_index("tm")
    each, chan = start_ref.shape
    width = emb_ref.shape[1]
    times = emb_ref.shape[0]
    block = times // n * each
    greet(["tm"])
    copies = spread("tm", lambda p: cond_ref.at[p], lambda m: conds.at[m], s1, r1)
    copies += spread("tm", lambda p: square_ref.at[p], lambda m: squares.at[m], s2, r2)
    conds[me] = cond_ref[me]
    squares[me] = square_ref[me]
    start = start_ref[...]
    for j in range(times):
        low[j * each : (j + 1) * each, :] = start
    for copy in copies:
        copy.wait()
    square = sum(squares[i][:, :1] for i in range(n))
    inverse = lax.rsqrt(square / model_width + 1e-06)
    condition = sum(conds[i] for i in range(n)) * inverse
    for j in range(times):
        base[j * each : (j + 1) * each, :] = condition + emb_ref[j : j + 1, :]
    tile = 512 if width % 512 == 0 else width
    tile_out = 384 if chan % 384 == 0 else chan

    def sweep(_, carry):
        flat = low[...].astype(BF16)

        def first(i, c):
            cols = pl.ds(pl.multiple_of(i * tile, LANES), tile)
            preact = jnp.dot(flat, in_ref[:, cols], preferred_element_type=F32) + base[:, cols]
            action[:, cols] = jax.nn.silu(preact).astype(BF16)
            return c

        lax.fori_loop(0, width // tile, first, 0)
        act = action[...]

        def second(i, c):
            cols = pl.ds(pl.multiple_of(i * tile_out, LANES), tile_out)
            drift = jnp.dot(act, head_ref[:, cols], preferred_element_type=F32)
            first_state = start_ref[:, cols]
            running = jnp.zeros_like(first_state)
            for j in range(times):
                rows = slice(j * each, (j + 1) * each)
                low[rows, cols] = first_state + running
                if j + 1 < times:
                    step = step_ref[j : j + 1, :1]
                    running = running + (step * drift[rows, :] + noise_ref[rows, cols])
            return c

        lax.fori_loop(0, chan // tile_out, second, 0)
        return carry

    lax.fori_loop(0, SWEEPS, sweep, 0)
    states[...] = low[...]
    out_ref[me] = states[rows_of(me, block), :]
    for copy in spread(
        "tm", lambda p: states.at[rows_of(p, block)], lambda m: out_ref.at[m], s3, r3
    ):
        copy.wait()


def sweeps(model_width, cond, square, start, embedding, step, noise, in_weight, head_out):
    n = lax.axis_size("tm")
    each, chan = start.shape
    times, width = embedding.shape
    return pl.pallas_call(
        functools.partial(sweep_kernel, model_width),
        out_shape=jax.ShapeDtypeStruct((n, times // n * each, chan), F32),
        in_specs=[VMEM] * 8,
        out_specs=VMEM,
        scratch_shapes=[
            pltpu.VMEM(cond.shape, F32),
            pltpu.VMEM(square.shape, F32),
            pltpu.VMEM((times * each, width), F32),
            pltpu.VMEM((times * each, chan), F32),
            pltpu.VMEM((times * each, chan), F32),
            pltpu.VMEM((times * each, width), BF16),
        ]
        + sems("tm", "tm", "tm"),
        compiler_params=comm_params(3),
    )(cond, square, start, embedding, step, noise, in_weight, head_out)


def time_terms(levels, hidden_width):
    half_width = hidden_width // 2
    frequencies = jnp.exp(-math.log(10000.0) * jnp.arange(half_width, dtype=F32) / half_width)
    angles = levels[:-1, None] * frequencies[None, :]
    embedding = jnp.concatenate([jnp.sin(angles), jnp.cos(angles)], axis=1)
    step_size = (levels[:-1] - levels[1:]) / 1000.0
    return (embedding, step_size, jnp.sqrt(step_size))


def shards(
    queries,
    cache_keys,
    cache_values,
    residual,
    out_weight,
    norm_gain,
    cond_weight,
    in_weight,
    head_out,
    start_state,
    noise_draws,
    positions,
    cache_length,
    plan,
):
    n = lax.axis_size("tm")
    when = lax.axis_index("tm")
    head_index = lax.axis_index("heads")
    model_width = norm_gain.shape[0] * n
    key_count = cache_keys.shape[0]
    row_each, time_each, chan = noise_draws.shape
    each = row_each // n
    times = time_each * n
    width = in_weight.shape[1]

    cond_all = lax.all_gather(cond_weight, "heads")

    pair = jnp.arange(HD, dtype=jnp.int32) // 2
    frequencies = jnp.exp(-math.log(10000.0) * 2.0 * pair.astype(F32) / HD)
    angles = positions.astype(F32)[:, None] * frequencies[None, :]
    valid = cache_length - when.astype(jnp.int32) * key_count
    out, stats = attend(
        queries, jnp.cos(angles), jnp.sin(angles), cache_keys, cache_values, valid
    )
    attended = merge(out, stats)
    partial = jnp.dot(attended, out_weight, preferred_element_type=F32).astype(BF16)

    noise = noise_draws.reshape(n, each, time_each, chan).transpose(0, 2, 1, 3)
    noise = noise.reshape(n, time_each * each, chan)
    own_rows = lax.dynamic_slice_in_dim(residual, head_index * row_each, row_each, 0)
    scaled, square, noise = hidden_rows(partial, own_rows, norm_gain[None, :], noise)

    cond = jnp.einsum("rk,hkc->rhc", scaled, cond_all, preferred_element_type=F32)
    cond = cond.reshape(n, each, width)
    embedding, step_size, noise_scale = time_terms(plan.astype(F32), width)
    noise_term = noise.astype(F32).reshape(times, each, chan) * noise_scale[:, None, None]
    start = lax.dynamic_slice_in_dim(start_state, when * each, each, 0)
    states = sweeps(
        model_width,
        cond,
        square.reshape(n, each, LANES),
        start,
        embedding,
        jnp.broadcast_to(step_size[:, None], (times, LANES)),
        noise_term.reshape(times * each, chan),
        in_weight,
        head_out,
    )
    states = states.reshape(n, time_each, each, chan).transpose(0, 2, 1, 3)
    return states.reshape(row_each, time_each, chan)


def solution(mesh):
    placed = (
        P("groups", "heads"),
        P(("groups", "tm"), "heads"),
        P(("groups", "tm"), "heads"),
        P("groups", "tm"),
        P("heads", "tm"),
        P("tm"),
        P("tm", "heads"),
        P(),
        P(),
        P(("groups", "heads"), None),
        P(("groups", "heads"), "tm", None),
        P("groups"),
        P("groups"),
        P(),
    )
    return jax.shard_map(
        shards,
        mesh=mesh,
        in_specs=placed,
        out_specs=P(("groups", "heads"), "tm", None),
        check_vma=False,
    )
```

```python
import functools
import math

import jax
import jax.numpy as jnp
from jax import lax
from jax.experimental import pallas as pl
from jax.experimental.pallas import tpu as pltpu
from jax.sharding import PartitionSpec as P

HD = 128
SWEEPS = 3
LANES = 128
HEADS_AT_ONCE = 8
F32 = jnp.float32
BF16 = jnp.bfloat16
VMEM = pl.BlockSpec(memory_space=pltpu.VMEM)
LIMIT = 56 * 1024 * 1024


def greet(axes):
    barrier = pltpu.get_barrier_semaphore()
    count = 0
    for axis in axes:
        n = lax.axis_size(axis)
        me = lax.axis_index(axis)
        for step in range(1, n):
            pl.semaphore_signal(
                barrier,
                inc=1,
                device_id={axis: lax.rem(me + step, n)},
                device_id_type=pl.DeviceIdType.MESH,
            )
        count += n - 1
    pl.semaphore_wait(barrier, count)


def spread(axis, source, target, send, recv):
    n = lax.axis_size(axis)
    me = lax.axis_index(axis)
    copies = []
    for step in range(1, n):
        partner = lax.rem(me + step, n)
        copy = pltpu.make_async_remote_copy(
            src_ref=source(partner),
            dst_ref=target(me),
            send_sem=send.at[step],
            recv_sem=recv.at[step],
            device_id={axis: partner},
            device_id_type=pl.DeviceIdType.MESH,
        )
        copies.append(copy)
    return copies


def launch(copies):
    for copy in copies:
        copy.start()
    return copies


def rows_of(index, size):
    return pl.ds(pl.multiple_of(index * size, size), size)


def attend_kernel(
    valid_ref, q_ref, cos_ref, sin_ref, k_ref, v_ref, out_ref,
    outs, sides, parts, stats, merged, s1, r1, s2, r2, s3, r3,
):
    group = pl.program_id(0)
    groups, rows, width = outs.shape
    n = lax.axis_size("tm")
    me = lax.axis_index("tm")
    each = rows // n
    half = LANES // 2
    mine = rows_of(me, each)

    def scatter(g):
        return spread(
            "tm", lambda p: sides.at[g, rows_of(p, each)], lambda m: stats.at[g, m],
            s1.at[g], r1.at[g],
        ) + spread(
            "tm", lambda p: outs.at[g, rows_of(p, each)], lambda m: parts.at[g, m],
            s2.at[g], r2.at[g],
        )

    def gather(g):
        return spread(
            "tm", lambda p: merged.at[g, mine], lambda m: merged.at[g, rows_of(m, each)],
            s3.at[g], r3.at[g],
        )

    def finish(copies):
        for copy in copies:
            copy.wait()

    def combine(g):
        finish(scatter(g))
        tops = [stats[g, i, :, :half] for i in range(n)]
        top = functools.reduce(jnp.maximum, tops)
        factors = [jnp.exp(t - top) for t in tops]
        denom = sum(stats[g, i, :, half:] * factors[i] for i in range(n))
        for head in range(width // HD):
            cols = slice(head * HD, (head + 1) * HD)
            lane = slice(head, head + 1)
            numer = sum(
                parts[g, i, :, cols].astype(F32) * factors[i][:, lane] for i in range(n)
            )
            merged[g, mine, cols] = (numer / denom[:, lane]).astype(BF16)
        launch(gather(g))

    @pl.when(group == 0)
    def _():
        greet(["tm"])

    lane = lax.broadcasted_iota(jnp.int32, (rows, HD), 1)
    even = lane % 2 == 0
    valid = lax.broadcasted_iota(jnp.int32, (rows, k_ref.shape[0]), 1) < valid_ref[0]
    side = jnp.zeros((rows, LANES), F32)
    for head in range(width // HD):
        cols = slice(head * HD, (head + 1) * HD)
        q = q_ref[:, cols].astype(F32)
        other = jnp.where(even, -pltpu.roll(q, HD - 1, 1), pltpu.roll(q, 1, 1))
        rotated = (q * cos_ref[...] + other * sin_ref[...]).astype(BF16)
        scores = lax.dot_general(
            rotated, k_ref[:, cols], (((1,), (1,)), ((), ())), preferred_element_type=F32
        ) * (1.0 / math.sqrt(HD))
        masked = jnp.where(valid, scores, F32(-1e30))
        top = jnp.max(masked, axis=1, keepdims=True)
        weights = jnp.where(valid, jnp.exp(masked - top), F32(0.0))
        total = jnp.sum(weights, axis=1, keepdims=True)
        outs[group, :, cols] = jnp.dot(
            weights.astype(BF16), v_ref[:, cols], preferred_element_type=F32
        ).astype(BF16)
        side = jnp.where(lane == head, top, jnp.where(lane == head + half, total, side))
    sides[group] = side
    launch(scatter(group))
    stats[group, me] = sides[group, mine, :]
    parts[group, me] = outs[group, mine, :]

    @pl.when(group > 0)
    def _():
        combine(group - 1)

    @pl.when(group == groups - 1)
    def _():
        combine(group)
        for g in range(groups):
            finish(gather(g))
            out_ref[:, g * width : (g + 1) * width] = merged[g]


def sems(*axes):
    return [pltpu.SemaphoreType.DMA((lax.axis_size(a),)) for a in axes for _ in range(2)]


def comm_params(ident):
    return pltpu.CompilerParams(
        collective_id=ident, has_side_effects=True, vmem_limit_bytes=LIMIT
    )


def attend(queries, cosine, sine, keys, values, valid):
    rows, width = queries.shape
    count = keys.shape[0]
    n = lax.axis_size("tm")
    part = HD * math.gcd(width // HD, HEADS_AT_ONCE)
    groups = width // part
    cut = lambda size: pl.BlockSpec((size, part), lambda g: (0, g))
    fixed = lambda size: pl.BlockSpec((rows, size), lambda g: (0, 0))
    sem = pltpu.SemaphoreType.DMA((groups, n))
    return pl.pallas_call(
        attend_kernel,
        grid=(groups,),
        in_specs=[
            pl.BlockSpec(memory_space=pltpu.SMEM),
            cut(rows), fixed(LANES), fixed(LANES), cut(count), cut(count),
        ],
        out_specs=fixed(width),
        out_shape=jax.ShapeDtypeStruct((rows, width), BF16),
        scratch_shapes=[
            pltpu.VMEM((groups, rows, part), BF16),
            pltpu.VMEM((groups, rows, LANES), F32),
            pltpu.VMEM((groups, n, rows // n, part), BF16),
            pltpu.VMEM((groups, n, rows // n, LANES), F32),
            pltpu.VMEM((groups, rows, part), BF16),
        ]
        + [sem] * 6,
        compiler_params=comm_params(1),
        cost_estimate=pl.CostEstimate(
            flops=4 * rows * count * width,
            bytes_accessed=4 * count * width,
            transcendentals=rows * count * (width // HD),
        ),
    )(valid, queries, cosine, sine, keys, values)


def hidden_kernel(
    part_ref, res_ref, gain_ref, noise_ref, scaled_ref, square_ref, got_ref, parts, s1, r1, s2, r2
):
    n = lax.axis_size("heads")
    me = lax.axis_index("heads")
    when = lax.axis_index("tm")
    each = res_ref.shape[0]
    greet(["heads", "tm"])
    copies = launch(
        spread("heads", lambda p: part_ref.at[rows_of(p, each)], lambda m: parts.at[m], s1, r1)
    )
    others = launch(
        spread("tm", lambda p: noise_ref.at[p], lambda m: got_ref.at[m], s2, r2)
    )
    parts[me] = part_ref[rows_of(me, each), :]
    got_ref[when] = noise_ref[when]
    for copy in copies:
        copy.wait()
    hidden = res_ref[...].astype(F32) + sum(parts[i].astype(F32) for i in range(n))
    squares = jnp.sum(hidden * hidden, axis=1, keepdims=True)
    square_ref[...] = jnp.broadcast_to(squares, square_ref.shape)
    scaled_ref[...] = (hidden * gain_ref[...]).astype(BF16)
    for copy in others:
        copy.wait()


def hidden_rows(partial, residual, gain, noise):
    n = lax.axis_size("heads")
    each, width = residual.shape
    return pl.pallas_call(
        hidden_kernel,
        out_shape=[
            jax.ShapeDtypeStruct((each, width), BF16),
            jax.ShapeDtypeStruct((each, LANES), F32),
            jax.ShapeDtypeStruct(noise.shape, noise.dtype),
        ],
        in_specs=[VMEM] * 4,
        out_specs=[VMEM] * 3,
        scratch_shapes=[pltpu.VMEM((n, each, width), BF16)] + sems("heads", "tm"),
        compiler_params=comm_params(2),
    )(partial, residual, gain, noise)


def sweep_kernel(
    model_width, cond_ref, square_ref, start_ref, emb_ref, step_ref, noise_ref, in_ref, head_ref,
    out_ref, conds, squares, base, states, low, action, s1, r1, s2, r2, s3, r3,
):
    n = lax.axis_size("tm")
    me = lax.axis_index("tm")
    each, chan = start_ref.shape
    width = emb_ref.shape[1]
    times = emb_ref.shape[0]
    block = times // n * each
    greet(["tm"])
    copies = launch(spread("tm", lambda p: cond_ref.at[p], lambda m: conds.at[m], s1, r1))
    copies += launch(
        spread("tm", lambda p: square_ref.at[p], lambda m: squares.at[m], s2, r2)
    )
    conds[me] = cond_ref[me]
    squares[me] = square_ref[me]
    start = start_ref[...]
    for j in range(times):
        low[j * each : (j + 1) * each, :] = start
    for copy in copies:
        copy.wait()
    square = sum(squares[i][:, :1] for i in range(n))
    inverse = lax.rsqrt(square / model_width + 1e-06)
    condition = sum(conds[i] for i in range(n)) * inverse
    for j in range(times):
        base[j * each : (j + 1) * each, :] = condition + emb_ref[j : j + 1, :]
    tile = 512 if width % 512 == 0 else width
    tile_out = 384 if chan % 384 == 0 else chan

    def sweep(_, carry):
        flat = low[...].astype(BF16)

        def first(i, c):
            cols = pl.ds(pl.multiple_of(i * tile, LANES), tile)
            preact = jnp.dot(flat, in_ref[:, cols], preferred_element_type=F32) + base[:, cols]
            action[:, cols] = jax.nn.silu(preact).astype(BF16)
            return c

        lax.fori_loop(0, width // tile, first, 0)
        act = action[...]

        def second(i, c):
            cols = pl.ds(pl.multiple_of(i * tile_out, LANES), tile_out)
            drift = jnp.dot(act, head_ref[:, cols], preferred_element_type=F32)
            first_state = start_ref[:, cols]
            running = jnp.zeros_like(first_state)
            for j in range(times):
                rows = slice(j * each, (j + 1) * each)
                low[rows, cols] = first_state + running
                if j + 1 < times:
                    step = step_ref[j : j + 1, :1]
                    running = running + (step * drift[rows, :] + noise_ref[rows, cols])
            return c

        lax.fori_loop(0, chan // tile_out, second, 0)
        return carry

    lax.fori_loop(0, SWEEPS, sweep, 0)
    states[...] = low[...]
    out_ref[me] = states[rows_of(me, block), :]
    for copy in launch(
        spread("tm", lambda p: states.at[rows_of(p, block)], lambda m: out_ref.at[m], s3, r3)
    ):
        copy.wait()


def sweeps(model_width, cond, square, start, embedding, step, noise, in_weight, head_out):
    n = lax.axis_size("tm")
    each, chan = start.shape
    times, width = embedding.shape
    return pl.pallas_call(
        functools.partial(sweep_kernel, model_width),
        out_shape=jax.ShapeDtypeStruct((n, times // n * each, chan), F32),
        in_specs=[VMEM] * 8,
        out_specs=VMEM,
        scratch_shapes=[
            pltpu.VMEM(cond.shape, F32),
            pltpu.VMEM(square.shape, F32),
            pltpu.VMEM((times * each, width), F32),
            pltpu.VMEM((times * each, chan), F32),
            pltpu.VMEM((times * each, chan), F32),
            pltpu.VMEM((times * each, width), BF16),
        ]
        + sems("tm", "tm", "tm"),
        compiler_params=comm_params(3),
    )(cond, square, start, embedding, step, noise, in_weight, head_out)


def time_terms(levels, hidden_width):
    half_width = hidden_width // 2
    frequencies = jnp.exp(-math.log(10000.0) * jnp.arange(half_width, dtype=F32) / half_width)
    angles = levels[:-1, None] * frequencies[None, :]
    embedding = jnp.concatenate([jnp.sin(angles), jnp.cos(angles)], axis=1)
    step_size = (levels[:-1] - levels[1:]) / 1000.0
    return (embedding, step_size, jnp.sqrt(step_size))


def shards(
    queries,
    cache_keys,
    cache_values,
    residual,
    out_weight,
    norm_gain,
    cond_weight,
    in_weight,
    head_out,
    start_state,
    noise_draws,
    positions,
    cache_length,
    plan,
):
    n = lax.axis_size("tm")
    when = lax.axis_index("tm")
    head_index = lax.axis_index("heads")
    model_width = norm_gain.shape[0] * n
    key_count = cache_keys.shape[0]
    row_each, time_each, chan = noise_draws.shape
    each = row_each // n
    times = time_each * n
    width = in_weight.shape[1]

    cond_all = lax.all_gather(cond_weight, "heads")

    pair = jnp.arange(HD, dtype=jnp.int32) // 2
    frequencies = jnp.exp(-math.log(10000.0) * 2.0 * pair.astype(F32) / HD)
    angles = positions.astype(F32)[:, None] * frequencies[None, :]
    valid = cache_length - when.astype(jnp.int32) * key_count
    attended = attend(
        queries, jnp.cos(angles), jnp.sin(angles), cache_keys, cache_values, valid
    )
    partial = jnp.dot(attended, out_weight, preferred_element_type=F32).astype(BF16)

    noise = noise_draws.reshape(n, each, time_each, chan).transpose(0, 2, 1, 3)
    noise = noise.reshape(n, time_each * each, chan)
    own_rows = lax.dynamic_slice_in_dim(residual, head_index * row_each, row_each, 0)
    scaled, square, noise = hidden_rows(partial, own_rows, norm_gain[None, :], noise)

    cond = jnp.einsum("rk,hkc->rhc", scaled, cond_all, preferred_element_type=F32)
    cond = cond.reshape(n, each, width)
    embedding, step_size, noise_scale = time_terms(plan.astype(F32), width)
    noise_term = noise.astype(F32).reshape(times, each, chan) * noise_scale[:, None, None]
    start = lax.dynamic_slice_in_dim(start_state, when * each, each, 0)
    states = sweeps(
        model_width,
        cond,
        square.reshape(n, each, LANES),
        start,
        embedding,
        jnp.broadcast_to(step_size[:, None], (times, LANES)),
        noise_term.reshape(times * each, chan),
        in_weight,
        head_out,
    )
    states = states.reshape(n, time_each, each, chan).transpose(0, 2, 1, 3)
    return states.reshape(row_each, time_each, chan)


def solution(mesh):
    placed = (
        P("groups", "heads"),
        P(("groups", "tm"), "heads"),
        P(("groups", "tm"), "heads"),
        P("groups", "tm"),
        P("heads", "tm"),
        P("tm"),
        P("tm", "heads"),
        P(),
        P(),
        P(("groups", "heads"), None),
        P(("groups", "heads"), "tm", None),
        P("groups"),
        P("groups"),
        P(),
    )
    return jax.shard_map(
        shards,
        mesh=mesh,
        in_specs=placed,
        out_specs=P(("groups", "heads"), "tm", None),
        check_vma=False,
    )
```

```python
import functools
import math

import jax
import jax.numpy as jnp
from jax import lax
from jax.experimental import pallas as pl
from jax.experimental.pallas import tpu as pltpu
from jax.sharding import PartitionSpec as P

HD = 128
SWEEPS = 3
LANES = 128
HEADS_AT_ONCE = 4
F32 = jnp.float32
BF16 = jnp.bfloat16
VMEM = pl.BlockSpec(memory_space=pltpu.VMEM)
LIMIT = 56 * 1024 * 1024


def greet(axes):
    barrier = pltpu.get_barrier_semaphore()
    count = 0
    for axis in axes:
        n = lax.axis_size(axis)
        me = lax.axis_index(axis)
        for step in range(1, n):
            pl.semaphore_signal(
                barrier,
                inc=1,
                device_id={axis: lax.rem(me + step, n)},
                device_id_type=pl.DeviceIdType.MESH,
            )
        count += n - 1
    pl.semaphore_wait(barrier, count)


def spread(axis, source, target, send, recv):
    n = lax.axis_size(axis)
    me = lax.axis_index(axis)
    copies = []
    for step in range(1, n):
        partner = lax.rem(me + step, n)
        copy = pltpu.make_async_remote_copy(
            src_ref=source(partner),
            dst_ref=target(me),
            send_sem=send.at[step],
            recv_sem=recv.at[step],
            device_id={axis: partner},
            device_id_type=pl.DeviceIdType.MESH,
        )
        copies.append(copy)
    return copies


def launch(copies):
    for copy in copies:
        copy.start()
    return copies


def rows_of(index, size):
    return pl.ds(pl.multiple_of(index * size, size), size)


def attend_kernel(
    valid_ref, q_ref, cos_ref, sin_ref, k_ref, v_ref, out_ref,
    outs, sides, parts, stats, turned, merged, s1, r1, s2, r2, s3, r3,
):
    group = pl.program_id(0)
    groups, rows, width = outs.shape
    n = lax.axis_size("tm")
    me = lax.axis_index("tm")
    each = rows // n
    count = width // HD
    mine = rows_of(me, each)

    def scatter(g):
        return spread(
            "tm", lambda p: sides.at[g], lambda m: stats.at[g, m],
            s1.at[g], r1.at[g],
        ) + spread(
            "tm", lambda p: outs.at[g, rows_of(p, each)], lambda m: parts.at[g, m],
            s2.at[g], r2.at[g],
        )

    def gather(g):
        return spread(
            "tm", lambda p: merged.at[g, mine], lambda m: merged.at[g, rows_of(m, each)],
            s3.at[g], r3.at[g],
        )

    def finish(copies):
        for copy in copies:
            copy.wait()

    def combine(g):
        finish(scatter(g))
        rest = jnp.zeros((LANES - stats.shape[2], rows), F32)
        for i in range(n):
            turned[i] = jnp.concatenate([stats[g, i], rest], axis=0).T
        tops = [turned[i, mine, :] for i in range(n)]
        top = functools.reduce(jnp.maximum, tops)
        factors = [jnp.exp(t - top) for t in tops]
        denom = sum(pltpu.roll(tops[i], LANES - count, 1) * factors[i] for i in range(n))
        for head in range(width // HD):
            cols = slice(head * HD, (head + 1) * HD)
            lane = slice(head, head + 1)
            numer = sum(
                parts[g, i, :, cols].astype(F32) * factors[i][:, lane] for i in range(n)
            )
            merged[g, mine, cols] = (numer / denom[:, lane]).astype(BF16)
        launch(gather(g))

    @pl.when(group == 0)
    def _():
        greet(["tm"])

    lane = lax.broadcasted_iota(jnp.int32, (rows, HD), 1)
    even = lane % 2 == 0
    valid = lax.broadcasted_iota(jnp.int32, (rows, k_ref.shape[0]), 1) < valid_ref[0]
    side = jnp.zeros((rows, LANES), F32)
    for head in range(width // HD):
        cols = slice(head * HD, (head + 1) * HD)
        q = q_ref[:, cols].astype(F32)
        other = jnp.where(even, -pltpu.roll(q, HD - 1, 1), pltpu.roll(q, 1, 1))
        rotated = (q * cos_ref[...] + other * sin_ref[...]).astype(BF16)
        scores = lax.dot_general(
            rotated, k_ref[:, cols], (((1,), (1,)), ((), ())), preferred_element_type=F32
        ) * (1.0 / math.sqrt(HD))
        masked = jnp.where(valid, scores, F32(-1e30))
        top = jnp.max(masked, axis=1, keepdims=True)
        weights = jnp.where(valid, jnp.exp(masked - top), F32(0.0))
        total = jnp.sum(weights, axis=1, keepdims=True)
        outs[group, :, cols] = jnp.dot(
            weights.astype(BF16), v_ref[:, cols], preferred_element_type=F32
        ).astype(BF16)
        side = jnp.where(lane == head, top, jnp.where(lane == head + count, total, side))
    sides[group] = side.T[: sides.shape[1], :]
    launch(scatter(group))
    stats[group, me] = sides[group]
    parts[group, me] = outs[group, mine, :]

    @pl.when(group > 0)
    def _():
        combine(group - 1)

    @pl.when(group == groups - 1)
    def _():
        combine(group)
        for g in range(groups):
            finish(gather(g))
            out_ref[:, g * width : (g + 1) * width] = merged[g]


def sems(*axes):
    return [pltpu.SemaphoreType.DMA((lax.axis_size(a),)) for a in axes for _ in range(2)]


def comm_params(ident):
    return pltpu.CompilerParams(
        collective_id=ident, has_side_effects=True, vmem_limit_bytes=LIMIT
    )


def attend(queries, cosine, sine, keys, values, valid):
    rows, width = queries.shape
    count = keys.shape[0]
    n = lax.axis_size("tm")
    part = HD * math.gcd(width // HD, HEADS_AT_ONCE)
    groups = width // part
    cut = lambda size: pl.BlockSpec((size, part), lambda g: (0, g))
    fixed = lambda size: pl.BlockSpec((rows, size), lambda g: (0, 0))
    sem = pltpu.SemaphoreType.DMA((groups, n))
    return pl.pallas_call(
        attend_kernel,
        grid=(groups,),
        in_specs=[
            pl.BlockSpec(memory_space=pltpu.SMEM),
            cut(rows), fixed(LANES), fixed(LANES), cut(count), cut(count),
        ],
        out_specs=fixed(width),
        out_shape=jax.ShapeDtypeStruct((rows, width), BF16),
        scratch_shapes=[
            pltpu.VMEM((groups, rows, part), BF16),
            pltpu.VMEM((groups, 2 * HEADS_AT_ONCE, rows), F32),
            pltpu.VMEM((groups, n, rows // n, part), BF16),
            pltpu.VMEM((groups, n, 2 * HEADS_AT_ONCE, rows), F32),
            pltpu.VMEM((n, rows, LANES), F32),
            pltpu.VMEM((groups, rows, part), BF16),
        ]
        + [sem] * 6,
        compiler_params=comm_params(1),
        cost_estimate=pl.CostEstimate(
            flops=4 * rows * count * width,
            bytes_accessed=4 * count * width,
            transcendentals=rows * count * (width // HD),
        ),
    )(valid, queries, cosine, sine, keys, values)


def hidden_kernel(
    part_ref, res_ref, gain_ref, noise_ref, scaled_ref, square_ref, got_ref, parts, s1, r1, s2, r2
):
    n = lax.axis_size("heads")
    me = lax.axis_index("heads")
    when = lax.axis_index("tm")
    each = res_ref.shape[0]
    greet(["heads", "tm"])
    copies = launch(
        spread("heads", lambda p: part_ref.at[rows_of(p, each)], lambda m: parts.at[m], s1, r1)
    )
    others = launch(
        spread("tm", lambda p: noise_ref.at[p], lambda m: got_ref.at[m], s2, r2)
    )
    parts[me] = part_ref[rows_of(me, each), :]
    got_ref[when] = noise_ref[when]
    for copy in copies:
        copy.wait()
    hidden = res_ref[...].astype(F32) + sum(parts[i].astype(F32) for i in range(n))
    squares = jnp.sum(hidden * hidden, axis=1, keepdims=True)
    square_ref[...] = jnp.broadcast_to(squares, square_ref.shape)
    scaled_ref[...] = (hidden * gain_ref[...]).astype(BF16)
    for copy in others:
        copy.wait()


def hidden_rows(partial, residual, gain, noise):
    n = lax.axis_size("heads")
    each, width = residual.shape
    return pl.pallas_call(
        hidden_kernel,
        out_shape=[
            jax.ShapeDtypeStruct((each, width), BF16),
            jax.ShapeDtypeStruct((each, LANES), F32),
            jax.ShapeDtypeStruct(noise.shape, noise.dtype),
        ],
        in_specs=[VMEM] * 4,
        out_specs=[VMEM] * 3,
        scratch_shapes=[pltpu.VMEM((n, each, width), BF16)] + sems("heads", "tm"),
        compiler_params=comm_params(2),
    )(partial, residual, gain, noise)


def sweep_kernel(
    model_width, cond_ref, square_ref, start_ref, emb_ref, step_ref, noise_ref, in_ref, head_ref,
    out_ref, conds, squares, base, states, low, action, s1, r1, s2, r2, s3, r3,
):
    n = lax.axis_size("tm")
    me = lax.axis_index("tm")
    each, chan = start_ref.shape
    width = emb_ref.shape[1]
    times = emb_ref.shape[0]
    block = times // n * each
    greet(["tm"])
    copies = launch(spread("tm", lambda p: cond_ref.at[p], lambda m: conds.at[m], s1, r1))
    copies += launch(
        spread("tm", lambda p: square_ref.at[p], lambda m: squares.at[m], s2, r2)
    )
    conds[me] = cond_ref[me]
    squares[me] = square_ref[me]
    start = start_ref[...]
    for j in range(times):
        low[j * each : (j + 1) * each, :] = start
    for copy in copies:
        copy.wait()
    square = sum(squares[i][:, :1] for i in range(n))
    inverse = lax.rsqrt(square / model_width + 1e-06)
    condition = sum(conds[i] for i in range(n)) * inverse
    for j in range(times):
        base[j * each : (j + 1) * each, :] = condition + emb_ref[j : j + 1, :]
    tile = 512 if width % 512 == 0 else width
    tile_out = 384 if chan % 384 == 0 else chan

    def sweep(_, carry):
        flat = low[...].astype(BF16)

        def first(i, c):
            cols = pl.ds(pl.multiple_of(i * tile, LANES), tile)
            preact = jnp.dot(flat, in_ref[:, cols], preferred_element_type=F32) + base[:, cols]
            action[:, cols] = jax.nn.silu(preact).astype(BF16)
            return c

        lax.fori_loop(0, width // tile, first, 0)
        act = action[...]

        def second(i, c):
            cols = pl.ds(pl.multiple_of(i * tile_out, LANES), tile_out)
            drift = jnp.dot(act, head_ref[:, cols], preferred_element_type=F32)
            first_state = start_ref[:, cols]
            running = jnp.zeros_like(first_state)
            for j in range(times):
                rows = slice(j * each, (j + 1) * each)
                low[rows, cols] = first_state + running
                if j + 1 < times:
                    step = step_ref[j : j + 1, :1]
                    running = running + (step * drift[rows, :] + noise_ref[rows, cols])
            return c

        lax.fori_loop(0, chan // tile_out, second, 0)
        return carry

    lax.fori_loop(0, SWEEPS, sweep, 0)
    change = (low[...] - jnp.concatenate([start] * times, axis=0)).astype(BF16)
    for i in range(n):
        states[i] = change[i * block : (i + 1) * block, :]
    out_ref[me] = states[me]
    for copy in launch(
        spread("tm", lambda p: states.at[p], lambda m: out_ref.at[m], s3, r3)
    ):
        copy.wait()


def sweeps(model_width, cond, square, start, embedding, step, noise, in_weight, head_out):
    n = lax.axis_size("tm")
    each, chan = start.shape
    times, width = embedding.shape
    return pl.pallas_call(
        functools.partial(sweep_kernel, model_width),
        out_shape=jax.ShapeDtypeStruct((n, times // n * each, chan), BF16),
        in_specs=[VMEM] * 8,
        out_specs=VMEM,
        scratch_shapes=[
            pltpu.VMEM(cond.shape, F32),
            pltpu.VMEM(square.shape, F32),
            pltpu.VMEM((times * each, width), F32),
            pltpu.VMEM((n, times // n * each, chan), BF16),
            pltpu.VMEM((times * each, chan), F32),
            pltpu.VMEM((times * each, width), BF16),
        ]
        + sems("tm", "tm", "tm"),
        compiler_params=comm_params(3),
    )(cond, square, start, embedding, step, noise, in_weight, head_out)


def time_terms(levels, hidden_width):
    half_width = hidden_width // 2
    frequencies = jnp.exp(-math.log(10000.0) * jnp.arange(half_width, dtype=F32) / half_width)
    angles = levels[:-1, None] * frequencies[None, :]
    embedding = jnp.concatenate([jnp.sin(angles), jnp.cos(angles)], axis=1)
    step_size = (levels[:-1] - levels[1:]) / 1000.0
    return (embedding, step_size, jnp.sqrt(step_size))


def shards(
    queries,
    cache_keys,
    cache_values,
    residual,
    out_weight,
    norm_gain,
    cond_weight,
    in_weight,
    head_out,
    start_state,
    noise_draws,
    positions,
    cache_length,
    plan,
):
    n = lax.axis_size("tm")
    when = lax.axis_index("tm")
    head_index = lax.axis_index("heads")
    model_width = norm_gain.shape[0] * n
    key_count = cache_keys.shape[0]
    row_each, time_each, chan = noise_draws.shape
    each = row_each // n
    times = time_each * n
    width = in_weight.shape[1]

    cond_all = lax.all_gather(cond_weight, "heads")

    pair = jnp.arange(HD, dtype=jnp.int32) // 2
    frequencies = jnp.exp(-math.log(10000.0) * 2.0 * pair.astype(F32) / HD)
    angles = positions.astype(F32)[:, None] * frequencies[None, :]
    valid = cache_length - when.astype(jnp.int32) * key_count
    attended = attend(
        queries, jnp.cos(angles), jnp.sin(angles), cache_keys, cache_values, valid
    )
    partial = jnp.dot(attended, out_weight, preferred_element_type=F32).astype(BF16)

    noise = noise_draws.reshape(n, each, time_each, chan).transpose(0, 2, 1, 3)
    noise = noise.reshape(n, time_each * each, chan)
    own_rows = lax.dynamic_slice_in_dim(residual, head_index * row_each, row_each, 0)
    scaled, square, noise = hidden_rows(partial, own_rows, norm_gain[None, :], noise)

    cond = jnp.einsum("rk,hkc->rhc", scaled, cond_all, preferred_element_type=F32)
    cond = cond.reshape(n, each, width)
    embedding, step_size, noise_scale = time_terms(plan.astype(F32), width)
    noise_term = noise.astype(F32).reshape(times, each, chan) * noise_scale[:, None, None]
    start = lax.dynamic_slice_in_dim(start_state, when * each, each, 0)
    change = sweeps(
        model_width,
        cond,
        square.reshape(n, each, LANES),
        start,
        embedding,
        jnp.broadcast_to(step_size[:, None], (times, LANES)),
        noise_term.reshape(times * each, chan),
        in_weight,
        head_out,
    )
    change = change.reshape(n, time_each, each, chan).transpose(0, 2, 1, 3)
    return start_state[:, None, :] + change.reshape(row_each, time_each, chan).astype(F32)


def solution(mesh):
    placed = (
        P("groups", "heads"),
        P(("groups", "tm"), "heads"),
        P(("groups", "tm"), "heads"),
        P("groups", "tm"),
        P("heads", "tm"),
        P("tm"),
        P("tm", "heads"),
        P(),
        P(),
        P(("groups", "heads"), None),
        P(("groups", "heads"), "tm", None),
        P("groups"),
        P("groups"),
        P(),
    )
    return jax.shard_map(
        shards,
        mesh=mesh,
        in_specs=placed,
        out_specs=P(("groups", "heads"), "tm", None),
        check_vma=False,
    )
```

```python
import functools
import math

import jax
import jax.numpy as jnp
from jax import lax
from jax.experimental import pallas as pl
from jax.experimental.pallas import tpu as pltpu
from jax.sharding import PartitionSpec as P

HD = 128
SWEEPS = 3
LANES = 128
HEADS_AT_ONCE = 4
F32 = jnp.float32
BF16 = jnp.bfloat16
VMEM = pl.BlockSpec(memory_space=pltpu.VMEM)
LIMIT = 56 * 1024 * 1024


def greet(axes):
    barrier = pltpu.get_barrier_semaphore()
    count = 0
    for axis in axes:
        n = lax.axis_size(axis)
        me = lax.axis_index(axis)
        for step in range(1, n):
            pl.semaphore_signal(
                barrier,
                inc=1,
                device_id={axis: lax.rem(me + step, n)},
                device_id_type=pl.DeviceIdType.MESH,
            )
        count += n - 1
    pl.semaphore_wait(barrier, count)


def spread(axis, source, target, send, recv):
    n = lax.axis_size(axis)
    me = lax.axis_index(axis)
    copies = []
    for step in range(1, n):
        partner = lax.rem(me + step, n)
        copy = pltpu.make_async_remote_copy(
            src_ref=source(partner),
            dst_ref=target(me),
            send_sem=send.at[step],
            recv_sem=recv.at[step],
            device_id={axis: partner},
            device_id_type=pl.DeviceIdType.MESH,
        )
        copies.append(copy)
    return copies


def launch(copies):
    for copy in copies:
        copy.start()
    return copies


def rows_of(index, size):
    return pl.ds(pl.multiple_of(index * size, size), size)


def attend_kernel(
    valid_ref, q_ref, cos_ref, sin_ref, k_ref, v_ref, out_ref,
    outs, sides, parts, stats, turned, merged, s1, r1, s2, r2, s3, r3,
):
    group = pl.program_id(0)
    groups, rows, width = outs.shape
    n = lax.axis_size("tm")
    me = lax.axis_index("tm")
    each = rows // n
    count = width // HD
    mine = rows_of(me, each)

    def scatter(g):
        return spread(
            "tm", lambda p: sides.at[g], lambda m: stats.at[g, m],
            s1.at[g], r1.at[g],
        ) + spread(
            "tm", lambda p: outs.at[g, rows_of(p, each)], lambda m: parts.at[g, m],
            s2.at[g], r2.at[g],
        )

    def gather(g):
        return spread(
            "tm", lambda p: merged.at[g, mine], lambda m: merged.at[g, rows_of(m, each)],
            s3.at[g], r3.at[g],
        )

    def finish(copies):
        for copy in copies:
            copy.wait()

    def combine(g):
        finish(scatter(g))
        rest = jnp.zeros((LANES - stats.shape[2], rows), F32)
        for i in range(n):
            turned[i] = jnp.concatenate([stats[g, i], rest], axis=0).T
        tops = [turned[i, mine, :] for i in range(n)]
        top = functools.reduce(jnp.maximum, tops)
        factors = [jnp.exp(t - top) for t in tops]
        denom = sum(pltpu.roll(tops[i], LANES - count, 1) * factors[i] for i in range(n))
        for head in range(width // HD):
            cols = slice(head * HD, (head + 1) * HD)
            lane = slice(head, head + 1)
            numer = sum(
                parts[g, i, :, cols].astype(F32) * factors[i][:, lane] for i in range(n)
            )
            merged[g, mine, cols] = (numer / denom[:, lane]).astype(BF16)
        launch(gather(g))

    @pl.when(group == 0)
    def _():
        greet(["tm"])

    lane = lax.broadcasted_iota(jnp.int32, (rows, HD), 1)
    even = lane % 2 == 0
    valid = lax.broadcasted_iota(jnp.int32, (rows, k_ref.shape[0]), 1) < valid_ref[0]
    side = jnp.zeros((rows, LANES), F32)
    for head in range(width // HD):
        cols = slice(head * HD, (head + 1) * HD)
        q = q_ref[:, cols].astype(F32)
        other = jnp.where(even, -pltpu.roll(q, HD - 1, 1), pltpu.roll(q, 1, 1))
        rotated = (q * cos_ref[...] + other * sin_ref[...]).astype(BF16)
        scores = lax.dot_general(
            rotated, k_ref[:, cols], (((1,), (1,)), ((), ())), preferred_element_type=F32
        ) * (1.0 / math.sqrt(HD))
        masked = jnp.where(valid, scores, F32(-1e30))
        top = jnp.max(masked, axis=1, keepdims=True)
        weights = jnp.where(valid, jnp.exp(masked - top), F32(0.0))
        total = jnp.sum(weights, axis=1, keepdims=True)
        outs[group, :, cols] = jnp.dot(
            weights.astype(BF16), v_ref[:, cols], preferred_element_type=F32
        ).astype(BF16)
        side = jnp.where(lane == head, top, jnp.where(lane == head + count, total, side))
    sides[group] = side.T[: sides.shape[1], :]
    launch(scatter(group))
    stats[group, me] = sides[group]
    parts[group, me] = outs[group, mine, :]

    @pl.when(group > 0)
    def _():
        combine(group - 1)

    @pl.when(group == groups - 1)
    def _():
        combine(group)
        for g in range(groups):
            finish(gather(g))
            out_ref[:, g * width : (g + 1) * width] = merged[g]


def sems(*axes):
    return [pltpu.SemaphoreType.DMA((lax.axis_size(a),)) for a in axes for _ in range(2)]


def comm_params(ident):
    return pltpu.CompilerParams(
        collective_id=ident, has_side_effects=True, vmem_limit_bytes=LIMIT
    )


def attend(queries, cosine, sine, keys, values, valid):
    rows, width = queries.shape
    count = keys.shape[0]
    n = lax.axis_size("tm")
    part = HD * math.gcd(width // HD, HEADS_AT_ONCE)
    groups = width // part
    cut = lambda size: pl.BlockSpec((size, part), lambda g: (0, g))
    fixed = lambda size: pl.BlockSpec((rows, size), lambda g: (0, 0))
    sem = pltpu.SemaphoreType.DMA((groups, n))
    return pl.pallas_call(
        attend_kernel,
        grid=(groups,),
        in_specs=[
            pl.BlockSpec(memory_space=pltpu.SMEM),
            cut(rows), fixed(LANES), fixed(LANES), cut(count), cut(count),
        ],
        out_specs=fixed(width),
        out_shape=jax.ShapeDtypeStruct((rows, width), BF16),
        scratch_shapes=[
            pltpu.VMEM((groups, rows, part), BF16),
            pltpu.VMEM((groups, 2 * HEADS_AT_ONCE, rows), F32),
            pltpu.VMEM((groups, n, rows // n, part), BF16),
            pltpu.VMEM((groups, n, 2 * HEADS_AT_ONCE, rows), F32),
            pltpu.VMEM((n, rows, LANES), F32),
            pltpu.VMEM((groups, rows, part), BF16),
        ]
        + [sem] * 6,
        compiler_params=comm_params(1),
        cost_estimate=pl.CostEstimate(
            flops=4 * rows * count * width,
            bytes_accessed=4 * count * width,
            transcendentals=rows * count * (width // HD),
        ),
    )(valid, queries, cosine, sine, keys, values)


def hidden_kernel(
    part_ref, res_ref, gain_ref, noise_ref, scaled_ref, square_ref, got_ref, parts, s1, r1, s2, r2
):
    n = lax.axis_size("heads")
    me = lax.axis_index("heads")
    when = lax.axis_index("tm")
    each = res_ref.shape[0]
    greet(["heads", "tm"])
    copies = launch(
        spread("heads", lambda p: part_ref.at[rows_of(p, each)], lambda m: parts.at[m], s1, r1)
    )
    others = launch(
        spread("tm", lambda p: noise_ref.at[p], lambda m: got_ref.at[m], s2, r2)
    )
    parts[me] = part_ref[rows_of(me, each), :]
    got_ref[when] = noise_ref[when]
    for copy in copies:
        copy.wait()
    hidden = res_ref[...].astype(F32) + sum(parts[i].astype(F32) for i in range(n))
    squares = jnp.sum(hidden * hidden, axis=1, keepdims=True)
    square_ref[...] = jnp.broadcast_to(squares, square_ref.shape)
    scaled_ref[...] = (hidden * gain_ref[...]).astype(BF16)
    for copy in others:
        copy.wait()


def hidden_rows(partial, residual, gain, noise):
    n = lax.axis_size("heads")
    each, width = residual.shape
    return pl.pallas_call(
        hidden_kernel,
        out_shape=[
            jax.ShapeDtypeStruct((each, width), BF16),
            jax.ShapeDtypeStruct((each, LANES), F32),
            jax.ShapeDtypeStruct(noise.shape, noise.dtype),
        ],
        in_specs=[VMEM] * 4,
        out_specs=[VMEM] * 3,
        scratch_shapes=[pltpu.VMEM((n, each, width), BF16)] + sems("heads", "tm"),
        compiler_params=comm_params(2),
    )(partial, residual, gain, noise)


def sweep_kernel(
    model_width, cond_ref, square_ref, start_ref, emb_ref, step_ref, noise_ref, in_hbm, head_hbm,
    out_ref, conds, squares, base, states, low, action, in_ref, head_ref, load,
    s1, r1, s2, r2, s3, r3,
):
    n = lax.axis_size("tm")
    me = lax.axis_index("tm")
    each, chan = start_ref.shape
    width = emb_ref.shape[1]
    times = emb_ref.shape[0]
    block = times // n * each
    loads = launch(
        [
            pltpu.make_async_copy(in_hbm, in_ref, load.at[0]),
            pltpu.make_async_copy(head_hbm, head_ref, load.at[1]),
        ]
    )
    greet(["tm"])
    copies = launch(spread("tm", lambda p: cond_ref.at[p], lambda m: conds.at[m], s1, r1))
    copies += launch(
        spread("tm", lambda p: square_ref.at[p], lambda m: squares.at[m], s2, r2)
    )
    conds[me] = cond_ref[me]
    squares[me] = square_ref[me]
    start = start_ref[...]
    for j in range(times):
        low[j * each : (j + 1) * each, :] = start
    for copy in copies:
        copy.wait()
    square = sum(squares[i][:, :1] for i in range(n))
    inverse = lax.rsqrt(square / model_width + 1e-06)
    condition = sum(conds[i] for i in range(n)) * inverse
    for j in range(times):
        base[j * each : (j + 1) * each, :] = condition + emb_ref[j : j + 1, :]
    for copy in loads:
        copy.wait()
    tile = 512 if width % 512 == 0 else width
    tile_out = 384 if chan % 384 == 0 else chan

    def sweep(_, carry):
        flat = low[...].astype(BF16)

        def first(i, c):
            cols = pl.ds(pl.multiple_of(i * tile, LANES), tile)
            preact = jnp.dot(flat, in_ref[:, cols], preferred_element_type=F32) + base[:, cols]
            action[:, cols] = jax.nn.silu(preact).astype(BF16)
            return c

        lax.fori_loop(0, width // tile, first, 0)
        act = action[...]

        def second(i, c):
            cols = pl.ds(pl.multiple_of(i * tile_out, LANES), tile_out)
            drift = jnp.dot(act, head_ref[:, cols], preferred_element_type=F32)
            first_state = start_ref[:, cols]
            running = jnp.zeros_like(first_state)
            for j in range(times):
                rows = slice(j * each, (j + 1) * each)
                low[rows, cols] = first_state + running
                if j + 1 < times:
                    step = step_ref[j : j + 1, :1]
                    running = running + (step * drift[rows, :] + noise_ref[rows, cols])
            return c

        lax.fori_loop(0, chan // tile_out, second, 0)
        return carry

    lax.fori_loop(0, SWEEPS, sweep, 0)
    change = (low[...] - jnp.concatenate([start] * times, axis=0)).astype(BF16)
    for i in range(n):
        states[i] = change[i * block : (i + 1) * block, :]
    out_ref[me] = states[me]
    for copy in launch(
        spread("tm", lambda p: states.at[p], lambda m: out_ref.at[m], s3, r3)
    ):
        copy.wait()


def sweeps(model_width, cond, square, start, embedding, step, noise, in_weight, head_out):
    n = lax.axis_size("tm")
    each, chan = start.shape
    times, width = embedding.shape
    return pl.pallas_call(
        functools.partial(sweep_kernel, model_width),
        out_shape=jax.ShapeDtypeStruct((n, times // n * each, chan), BF16),
        in_specs=[VMEM] * 6 + [pl.BlockSpec(memory_space=pl.ANY)] * 2,
        out_specs=VMEM,
        scratch_shapes=[
            pltpu.VMEM(cond.shape, F32),
            pltpu.VMEM(square.shape, F32),
            pltpu.VMEM((times * each, width), F32),
            pltpu.VMEM((n, times // n * each, chan), BF16),
            pltpu.VMEM((times * each, chan), F32),
            pltpu.VMEM((times * each, width), BF16),
            pltpu.VMEM(in_weight.shape, BF16),
            pltpu.VMEM(head_out.shape, BF16),
            pltpu.SemaphoreType.DMA((2,)),
        ]
        + sems("tm", "tm", "tm"),
        compiler_params=comm_params(3),
    )(cond, square, start, embedding, step, noise, in_weight, head_out)


def time_terms(levels, hidden_width):
    half_width = hidden_width // 2
    frequencies = jnp.exp(-math.log(10000.0) * jnp.arange(half_width, dtype=F32) / half_width)
    angles = levels[:-1, None] * frequencies[None, :]
    embedding = jnp.concatenate([jnp.sin(angles), jnp.cos(angles)], axis=1)
    step_size = (levels[:-1] - levels[1:]) / 1000.0
    return (embedding, step_size, jnp.sqrt(step_size))


def shards(
    queries,
    cache_keys,
    cache_values,
    residual,
    out_weight,
    norm_gain,
    cond_weight,
    in_weight,
    head_out,
    start_state,
    noise_draws,
    positions,
    cache_length,
    plan,
):
    n = lax.axis_size("tm")
    when = lax.axis_index("tm")
    head_index = lax.axis_index("heads")
    model_width = norm_gain.shape[0] * n
    key_count = cache_keys.shape[0]
    row_each, time_each, chan = noise_draws.shape
    each = row_each // n
    times = time_each * n
    width = in_weight.shape[1]

    cond_all = lax.all_gather(cond_weight, "heads")

    pair = jnp.arange(HD, dtype=jnp.int32) // 2
    frequencies = jnp.exp(-math.log(10000.0) * 2.0 * pair.astype(F32) / HD)
    angles = positions.astype(F32)[:, None] * frequencies[None, :]
    valid = cache_length - when.astype(jnp.int32) * key_count
    attended = attend(
        queries, jnp.cos(angles), jnp.sin(angles), cache_keys, cache_values, valid
    )
    partial = jnp.dot(attended, out_weight, preferred_element_type=F32).astype(BF16)

    noise = noise_draws.reshape(n, each, time_each, chan).transpose(0, 2, 1, 3)
    noise = noise.reshape(n, time_each * each, chan)
    own_rows = lax.dynamic_slice_in_dim(residual, head_index * row_each, row_each, 0)
    scaled, square, noise = hidden_rows(partial, own_rows, norm_gain[None, :], noise)

    cond = jnp.einsum("rk,hkc->rhc", scaled, cond_all, preferred_element_type=F32)
    cond = cond.reshape(n, each, width)
    embedding, step_size, noise_scale = time_terms(plan.astype(F32), width)
    noise_term = noise.astype(F32).reshape(times, each, chan) * noise_scale[:, None, None]
    start = lax.dynamic_slice_in_dim(start_state, when * each, each, 0)
    change = sweeps(
        model_width,
        cond,
        square.reshape(n, each, LANES),
        start,
        embedding,
        jnp.broadcast_to(step_size[:, None], (times, LANES)),
        noise_term.reshape(times * each, chan),
        in_weight,
        head_out,
    )
    change = change.reshape(n, time_each, each, chan).transpose(0, 2, 1, 3)
    return start_state[:, None, :] + change.reshape(row_each, time_each, chan).astype(F32)


def solution(mesh):
    placed = (
        P("groups", "heads"),
        P(("groups", "tm"), "heads"),
        P(("groups", "tm"), "heads"),
        P("groups", "tm"),
        P("heads", "tm"),
        P("tm"),
        P("tm", "heads"),
        P(),
        P(),
        P(("groups", "heads"), None),
        P(("groups", "heads"), "tm", None),
        P("groups"),
        P("groups"),
        P(),
    )
    return jax.shard_map(
        shards,
        mesh=mesh,
        in_specs=placed,
        out_specs=P(("groups", "heads"), "tm", None),
        check_vma=False,
    )
```

```python
import functools
import math

import jax
import jax.numpy as jnp
from jax import lax
from jax.experimental import pallas as pl
from jax.experimental.pallas import tpu as pltpu
from jax.sharding import PartitionSpec as P

HD = 128
SWEEPS = 3
LANES = 128
HEADS_AT_ONCE = 4
F32 = jnp.float32
BF16 = jnp.bfloat16
VMEM = pl.BlockSpec(memory_space=pltpu.VMEM)
LIMIT = 56 * 1024 * 1024


def greet(axes):
    barrier = pltpu.get_barrier_semaphore()
    count = 0
    for axis in axes:
        n = lax.axis_size(axis)
        me = lax.axis_index(axis)
        for step in range(1, n):
            pl.semaphore_signal(
                barrier,
                inc=1,
                device_id={axis: lax.rem(me + step, n)},
                device_id_type=pl.DeviceIdType.MESH,
            )
        count += n - 1
    pl.semaphore_wait(barrier, count)


def spread(axis, source, target, send, recv):
    n = lax.axis_size(axis)
    me = lax.axis_index(axis)
    copies = []
    for step in range(1, n):
        partner = lax.rem(me + step, n)
        copy = pltpu.make_async_remote_copy(
            src_ref=source(partner),
            dst_ref=target(me),
            send_sem=send.at[step],
            recv_sem=recv.at[step],
            device_id={axis: partner},
            device_id_type=pl.DeviceIdType.MESH,
        )
        copies.append(copy)
    return copies


def launch(copies):
    for copy in copies:
        copy.start()
    return copies


def rows_of(index, size):
    return pl.ds(pl.multiple_of(index * size, size), size)


def attend_kernel(
    valid_ref, q_ref, cos_ref, sin_ref, k_ref, v_ref, out_ref,
    outs, sides, parts, stats, turned, merged, s1, r1, s2, r2, s3, r3,
):
    group = pl.program_id(0)
    groups, rows, width = outs.shape
    n = lax.axis_size("tm")
    me = lax.axis_index("tm")
    each = rows // n
    count = width // HD
    mine = rows_of(me, each)

    def scatter(g):
        return spread(
            "tm", lambda p: sides.at[g], lambda m: stats.at[g, m],
            s1.at[g], r1.at[g],
        ) + spread(
            "tm", lambda p: outs.at[g, rows_of(p, each)], lambda m: parts.at[g, m],
            s2.at[g], r2.at[g],
        )

    def gather(g):
        return spread(
            "tm", lambda p: merged.at[g, mine], lambda m: merged.at[g, rows_of(m, each)],
            s3.at[g], r3.at[g],
        )

    def finish(copies):
        for copy in copies:
            copy.wait()

    def combine(g):
        finish(scatter(g))
        rest = jnp.zeros((LANES - stats.shape[2], rows), F32)
        for i in range(n):
            turned[i] = jnp.concatenate([stats[g, i], rest], axis=0).T
        tops = [turned[i, mine, :] for i in range(n)]
        top = functools.reduce(jnp.maximum, tops)
        factors = [jnp.exp(t - top) for t in tops]
        denom = sum(pltpu.roll(tops[i], LANES - count, 1) * factors[i] for i in range(n))
        for head in range(width // HD):
            cols = slice(head * HD, (head + 1) * HD)
            lane = slice(head, head + 1)
            numer = sum(
                parts[g, i, :, cols].astype(F32) * factors[i][:, lane] for i in range(n)
            )
            merged[g, mine, cols] = (numer / denom[:, lane]).astype(BF16)
        launch(gather(g))

    @pl.when(group == 0)
    def _():
        greet(["tm"])

    lane = lax.broadcasted_iota(jnp.int32, (rows, HD), 1)
    even = lane % 2 == 0
    valid = lax.broadcasted_iota(jnp.int32, (rows, k_ref.shape[0]), 1) < valid_ref[0]
    side = jnp.zeros((rows, LANES), F32)
    for head in range(width // HD):
        cols = slice(head * HD, (head + 1) * HD)
        q = q_ref[:, cols].astype(F32)
        other = jnp.where(even, -pltpu.roll(q, HD - 1, 1), pltpu.roll(q, 1, 1))
        rotated = (q * cos_ref[...] + other * sin_ref[...]).astype(BF16)
        scores = lax.dot_general(
            rotated, k_ref[:, cols], (((1,), (1,)), ((), ())), preferred_element_type=F32
        ) * (1.0 / math.sqrt(HD))
        masked = jnp.where(valid, scores, F32(-1e30))
        top = jnp.max(masked, axis=1, keepdims=True)
        weights = jnp.exp(masked - jnp.maximum(top, F32(-1e29)))
        total = jnp.sum(weights, axis=1, keepdims=True)
        outs[group, :, cols] = jnp.dot(
            weights.astype(BF16), v_ref[:, cols], preferred_element_type=F32
        ).astype(BF16)
        side = jnp.where(lane == head, top, jnp.where(lane == head + count, total, side))
    sides[group] = side.T[: sides.shape[1], :]
    launch(scatter(group))
    stats[group, me] = sides[group]
    parts[group, me] = outs[group, mine, :]

    @pl.when(group > 0)
    def _():
        combine(group - 1)

    @pl.when(group == groups - 1)
    def _():
        combine(group)
        for g in range(groups):
            finish(gather(g))
            out_ref[:, g * width : (g + 1) * width] = merged[g]


def sems(*axes):
    return [pltpu.SemaphoreType.DMA((lax.axis_size(a),)) for a in axes for _ in range(2)]


def comm_params(ident):
    return pltpu.CompilerParams(
        collective_id=ident, has_side_effects=True, vmem_limit_bytes=LIMIT
    )


def attend(queries, cosine, sine, keys, values, valid):
    rows, width = queries.shape
    count = keys.shape[0]
    n = lax.axis_size("tm")
    part = HD * math.gcd(width // HD, HEADS_AT_ONCE)
    groups = width // part
    cut = lambda size: pl.BlockSpec((size, part), lambda g: (0, g))
    fixed = lambda size: pl.BlockSpec((rows, size), lambda g: (0, 0))
    sem = pltpu.SemaphoreType.DMA((groups, n))
    return pl.pallas_call(
        attend_kernel,
        grid=(groups,),
        in_specs=[
            pl.BlockSpec(memory_space=pltpu.SMEM),
            cut(rows), fixed(LANES), fixed(LANES), cut(count), cut(count),
        ],
        out_specs=fixed(width),
        out_shape=jax.ShapeDtypeStruct((rows, width), BF16),
        scratch_shapes=[
            pltpu.VMEM((groups, rows, part), BF16),
            pltpu.VMEM((groups, 2 * HEADS_AT_ONCE, rows), F32),
            pltpu.VMEM((groups, n, rows // n, part), BF16),
            pltpu.VMEM((groups, n, 2 * HEADS_AT_ONCE, rows), F32),
            pltpu.VMEM((n, rows, LANES), F32),
            pltpu.VMEM((groups, rows, part), BF16),
        ]
        + [sem] * 6,
        compiler_params=comm_params(1),
        cost_estimate=pl.CostEstimate(
            flops=4 * rows * count * width,
            bytes_accessed=4 * count * width,
            transcendentals=rows * count * (width // HD),
        ),
    )(valid, queries, cosine, sine, keys, values)


def hidden_kernel(
    part_ref, res_ref, gain_ref, noise_ref, scaled_ref, square_ref, got_ref, parts, s1, r1, s2, r2
):
    n = lax.axis_size("heads")
    me = lax.axis_index("heads")
    when = lax.axis_index("tm")
    each = res_ref.shape[0]
    greet(["heads", "tm"])
    copies = launch(
        spread("heads", lambda p: part_ref.at[rows_of(p, each)], lambda m: parts.at[m], s1, r1)
    )
    others = launch(
        spread("tm", lambda p: noise_ref.at[p], lambda m: got_ref.at[m], s2, r2)
    )
    parts[me] = part_ref[rows_of(me, each), :]
    got_ref[when] = noise_ref[when]
    for copy in copies:
        copy.wait()
    hidden = res_ref[...].astype(F32) + sum(parts[i].astype(F32) for i in range(n))
    squares = jnp.sum(hidden * hidden, axis=1, keepdims=True)
    square_ref[...] = jnp.broadcast_to(squares, square_ref.shape)
    scaled_ref[...] = (hidden * gain_ref[...]).astype(BF16)
    for copy in others:
        copy.wait()


def hidden_rows(partial, residual, gain, noise):
    n = lax.axis_size("heads")
    each, width = residual.shape
    return pl.pallas_call(
        hidden_kernel,
        out_shape=[
            jax.ShapeDtypeStruct((each, width), BF16),
            jax.ShapeDtypeStruct((each, LANES), F32),
            jax.ShapeDtypeStruct(noise.shape, noise.dtype),
        ],
        in_specs=[VMEM] * 4,
        out_specs=[VMEM] * 3,
        scratch_shapes=[pltpu.VMEM((n, each, width), BF16)] + sems("heads", "tm"),
        compiler_params=comm_params(2),
    )(partial, residual, gain, noise)


def sweep_kernel(
    model_width, cond_ref, square_ref, start_ref, emb_ref, step_ref, noise_ref, in_hbm, head_hbm,
    out_ref, conds, squares, base, states, low, action, in_ref, head_ref, load,
    s1, r1, s2, r2, s3, r3,
):
    n = lax.axis_size("tm")
    me = lax.axis_index("tm")
    each, chan = start_ref.shape
    width = emb_ref.shape[1]
    times = emb_ref.shape[0]
    block = times // n * each
    loads = launch(
        [
            pltpu.make_async_copy(in_hbm, in_ref, load.at[0]),
            pltpu.make_async_copy(head_hbm, head_ref, load.at[1]),
        ]
    )
    greet(["tm"])
    copies = launch(spread("tm", lambda p: cond_ref.at[p], lambda m: conds.at[m], s1, r1))
    copies += launch(
        spread("tm", lambda p: square_ref.at[p], lambda m: squares.at[m], s2, r2)
    )
    conds[me] = cond_ref[me]
    squares[me] = square_ref[me]
    start = start_ref[...]
    for j in range(times):
        low[j * each : (j + 1) * each, :] = start
    for copy in copies:
        copy.wait()
    square = sum(squares[i][:, :1] for i in range(n))
    inverse = lax.rsqrt(square / model_width + 1e-06)
    condition = sum(conds[i] for i in range(n)) * inverse
    for j in range(times):
        base[j * each : (j + 1) * each, :] = condition + emb_ref[j : j + 1, :]
    for copy in loads:
        copy.wait()
    tile = 512 if width % 512 == 0 else width
    tile_out = 384 if chan % 384 == 0 else chan

    def sweep(_, carry):
        flat = low[...].astype(BF16)

        def first(i, c):
            cols = pl.ds(pl.multiple_of(i * tile, LANES), tile)
            preact = jnp.dot(flat, in_ref[:, cols], preferred_element_type=F32) + base[:, cols]
            action[:, cols] = jax.nn.silu(preact).astype(BF16)
            return c

        lax.fori_loop(0, width // tile, first, 0)
        act = action[...]

        def second(i, c):
            cols = pl.ds(pl.multiple_of(i * tile_out, LANES), tile_out)
            drift = jnp.dot(act, head_ref[:, cols], preferred_element_type=F32)
            first_state = start_ref[:, cols]
            running = jnp.zeros_like(first_state)
            for j in range(times):
                rows = slice(j * each, (j + 1) * each)
                low[rows, cols] = first_state + running
                if j + 1 < times:
                    step = step_ref[j : j + 1, :1]
                    running = running + (step * drift[rows, :] + noise_ref[rows, cols])
            return c

        lax.fori_loop(0, chan // tile_out, second, 0)
        return carry

    lax.fori_loop(0, SWEEPS, sweep, 0)
    change = (low[...] - jnp.concatenate([start] * times, axis=0)).astype(BF16)
    for i in range(n):
        states[i] = change[i * block : (i + 1) * block, :]
    out_ref[me] = states[me]
    for copy in launch(
        spread("tm", lambda p: states.at[p], lambda m: out_ref.at[m], s3, r3)
    ):
        copy.wait()


def sweeps(model_width, cond, square, start, embedding, step, noise, in_weight, head_out):
    n = lax.axis_size("tm")
    each, chan = start.shape
    times, width = embedding.shape
    return pl.pallas_call(
        functools.partial(sweep_kernel, model_width),
        out_shape=jax.ShapeDtypeStruct((n, times // n * each, chan), BF16),
        in_specs=[VMEM] * 6 + [pl.BlockSpec(memory_space=pl.ANY)] * 2,
        out_specs=VMEM,
        scratch_shapes=[
            pltpu.VMEM(cond.shape, F32),
            pltpu.VMEM(square.shape, F32),
            pltpu.VMEM((times * each, width), F32),
            pltpu.VMEM((n, times // n * each, chan), BF16),
            pltpu.VMEM((times * each, chan), F32),
            pltpu.VMEM((times * each, width), BF16),
            pltpu.VMEM(in_weight.shape, BF16),
            pltpu.VMEM(head_out.shape, BF16),
            pltpu.SemaphoreType.DMA((2,)),
        ]
        + sems("tm", "tm", "tm"),
        compiler_params=comm_params(3),
    )(cond, square, start, embedding, step, noise, in_weight, head_out)


def time_terms(levels, hidden_width):
    half_width = hidden_width // 2
    frequencies = jnp.exp(-math.log(10000.0) * jnp.arange(half_width, dtype=F32) / half_width)
    angles = levels[:-1, None] * frequencies[None, :]
    embedding = jnp.concatenate([jnp.sin(angles), jnp.cos(angles)], axis=1)
    step_size = (levels[:-1] - levels[1:]) / 1000.0
    return (embedding, step_size, jnp.sqrt(step_size))


def shards(
    queries,
    cache_keys,
    cache_values,
    residual,
    out_weight,
    norm_gain,
    cond_weight,
    in_weight,
    head_out,
    start_state,
    noise_draws,
    positions,
    cache_length,
    plan,
):
    n = lax.axis_size("tm")
    when = lax.axis_index("tm")
    head_index = lax.axis_index("heads")
    model_width = norm_gain.shape[0] * n
    key_count = cache_keys.shape[0]
    row_each, time_each, chan = noise_draws.shape
    each = row_each // n
    times = time_each * n
    width = in_weight.shape[1]

    cond_all = lax.all_gather(cond_weight, "heads")

    pair = jnp.arange(HD, dtype=jnp.int32) // 2
    frequencies = jnp.exp(-math.log(10000.0) * 2.0 * pair.astype(F32) / HD)
    angles = positions.astype(F32)[:, None] * frequencies[None, :]
    valid = cache_length - when.astype(jnp.int32) * key_count
    attended = attend(
        queries, jnp.cos(angles), jnp.sin(angles), cache_keys, cache_values, valid
    )
    partial = jnp.dot(attended, out_weight, preferred_element_type=F32).astype(BF16)

    noise = noise_draws.reshape(n, each, time_each, chan).transpose(0, 2, 1, 3)
    noise = noise.reshape(n, time_each * each, chan)
    own_rows = lax.dynamic_slice_in_dim(residual, head_index * row_each, row_each, 0)
    scaled, square, noise = hidden_rows(partial, own_rows, norm_gain[None, :], noise)

    cond = jnp.einsum("rk,hkc->rhc", scaled, cond_all, preferred_element_type=F32)
    cond = cond.reshape(n, each, width)
    embedding, step_size, noise_scale = time_terms(plan.astype(F32), width)
    noise_term = noise.astype(F32).reshape(times, each, chan) * noise_scale[:, None, None]
    start = lax.dynamic_slice_in_dim(start_state, when * each, each, 0)
    change = sweeps(
        model_width,
        cond,
        square.reshape(n, each, LANES),
        start,
        embedding,
        jnp.broadcast_to(step_size[:, None], (times, LANES)),
        noise_term.reshape(times * each, chan),
        in_weight,
        head_out,
    )
    change = change.reshape(n, time_each, each, chan).transpose(0, 2, 1, 3)
    return start_state[:, None, :] + change.reshape(row_each, time_each, chan).astype(F32)


def solution(mesh):
    placed = (
        P("groups", "heads"),
        P(("groups", "tm"), "heads"),
        P(("groups", "tm"), "heads"),
        P("groups", "tm"),
        P("heads", "tm"),
        P("tm"),
        P("tm", "heads"),
        P(),
        P(),
        P(("groups", "heads"), None),
        P(("groups", "heads"), "tm", None),
        P("groups"),
        P("groups"),
        P(),
    )
    return jax.shard_map(
        shards,
        mesh=mesh,
        in_specs=placed,
        out_specs=P(("groups", "heads"), "tm", None),
        check_vma=False,
    )
```
